256 devices in a mesh: frame: 32 (over z, x), pos: 8 (over y, core).
Axes of the slice: x: 4, y: 4, z: 8, core: 2. Of those that a mesh axis runs over, the one named last changes fastest.
Arguments:
- qkv: bfloat16 [3, 32, 1536, 3072], P(None, 'frame', 'pos'), may hold values from -24 to 24
- head_kind: int32 [24], replicated, may hold values from 0 to 1, as said below
- out_weight: bfloat16 [3072, 3072], P(('frame', 'pos')), may hold values from -0.109375 to 0.109375
Outputs:
- projected: bfloat16 [32, 1536, 3072], P('frame', 'pos')
The draws below stay inside these ranges and needn't reach their ends.
Inputs may be any that keep to these rules, and one draw needn't show every extreme that they name: `head_kind`: exactly 16 entries are 0 and 8 entries are 1.
All inputs are finite; a program needn't handle non-finite values.
Results may differ from the reference program's by a relative error of at most 0.0065.
Values may be sent and summed in bfloat16 or wider, within the bound.
No kernel may reach another device: no remote copies, remote signals or barrier semaphores. Data moves between devices by JAX's collectives and lax.ppermute only.
A program may use at most 128 MiB of HBM per device.

```python
import jax
import jax.numpy as jnp
from jax import lax

HEADS = 24
HEAD_SIZE = 128
SPATIAL = 16
D = 3072
FRAMES = 32
POSITIONS = 1536


def draw_qkv(key, part):
    key = jax.random.fold_in(key, 11)
    key_one, key_two, key_three = jax.random.split(key, 3)
    extent = (FRAMES, POSITIONS, D)
    query_matrix = jnp.clip(2.0 * jax.random.normal(key_one, extent, jnp.float32), -8.0, 8.0)
    key_matrix = jnp.clip(2.0 * jax.random.normal(key_two, extent, jnp.float32), -8.0, 8.0)
    value_matrix = jnp.clip(jax.random.normal(key_three, extent, jnp.float32), -4.0, 4.0)
    return jnp.stack([query_matrix, key_matrix, value_matrix], axis=0).astype(jnp.bfloat16)


def draw_head_kind(key, part):
    key = jax.random.fold_in(key, 23)
    shuffled = jax.random.permutation(key, HEADS)
    return (shuffled >= SPATIAL).astype(jnp.int32)


def steps_of(own_key, dims, cuts, least, top_value):
    def one(position, parts):
        draws = jax.random.uniform(jax.random.fold_in(jax.random.fold_in(own_key, 6), position), (parts,), jnp.float32, least / len(cuts), top_value / len(cuts))
        return jnp.repeat(jnp.exp(draws), dims[position] // parts).reshape((-1,) + (1,) * (len(dims) - position - 1))

    level = one(*cuts[0])
    for cut in cuts[1:]:
        level = level * one(*cut)
    return level


def scatter_about(own_key, shape, spread, reach, pieces=(), dtype=jnp.bfloat16):
    values = spread * jax.random.normal(own_key, shape, jnp.float32)
    if pieces:
        values = values * steps_of(own_key, shape, pieces, -0.22, 0.18)
    return jnp.clip(values, -reach, reach).astype(dtype)


def setup_inputs(seed: int = 0) -> dict:
    streams_of = jax.random.split(jax.random.key(seed), 4)
    return {
        "qkv": draw_qkv(jax.random.fold_in(streams_of[3], 71), 0),
        "head_kind": draw_head_kind(jax.random.fold_in(streams_of[3], 71), 0),
        "out_weight": scatter_about(streams_of[2], (D, D), D ** -0.5, 0.109375, ((0, 256),)),
    }


def attend(query_matrix, key_matrix, value_matrix):
    score_matrix = jnp.einsum("nyw,nzw->nyz", query_matrix.astype(jnp.float32), key_matrix.astype(jnp.float32)) * (HEAD_SIZE ** -0.5)
    top_score = jnp.max(score_matrix, axis=-1, keepdims=True)
    expon = jnp.exp(score_matrix - top_score)
    totals = jnp.sum(expon, axis=-1, keepdims=True)
    softmax_weights = lax.optimization_barrier(expon.astype(jnp.bfloat16)).astype(jnp.float32)
    summed_values = jnp.einsum("vnm,vml->vnl", softmax_weights, value_matrix.astype(jnp.float32))
    return (summed_values / totals).astype(jnp.bfloat16)


def reference(qkv, head_kind, out_weight):
    stacked = qkv.reshape(3, FRAMES, POSITIONS, HEADS, HEAD_SIZE)
    ranking = jnp.argsort(head_kind, stable=True).astype(jnp.int32)
    spatial_ids = ranking[:SPATIAL]
    temporal_ids = ranking[SPATIAL:]
    spatial_in = jnp.transpose(jnp.take(stacked, spatial_ids, axis=3), (3, 0, 1, 2, 4))

    def spatial_head(block):
        per_frame = jnp.transpose(block, (1, 0, 2, 3))
        return lax.map(lambda frame_data: attend(frame_data[0][None], frame_data[1][None], frame_data[2][None])[0], per_frame)

    spatial_out = lax.map(spatial_head, spatial_in)
    temporal_in = jnp.transpose(jnp.take(stacked, temporal_ids, axis=3), (3, 0, 2, 1, 4))
    temporal_out = lax.map(lambda block: attend(block[0], block[1], block[2]), temporal_in)
    head_outputs = jnp.zeros((FRAMES, POSITIONS, HEADS, HEAD_SIZE), jnp.bfloat16)
    head_outputs = head_outputs.at[:, :, spatial_ids].set(jnp.transpose(spatial_out, (1, 2, 0, 3)))
    head_outputs = head_outputs.at[:, :, temporal_ids].set(jnp.transpose(temporal_out, (2, 1, 0, 3)))
    flat = head_outputs.reshape(FRAMES * POSITIONS, D)
    projected = jnp.dot(flat, out_weight, preferred_element_type=jnp.float32).astype(jnp.bfloat16)
    return projected.reshape(FRAMES, POSITIONS, D)
```

```python
import jax
import jax.numpy as jnp
from jax import lax
from jax.experimental import pallas as pl
from jax.experimental.pallas import tpu as pltpu
from jax.sharding import Mesh, PartitionSpec as P

HEADS = 24
SIZE = 128
SPATIAL = 16
D = 3072
FRAMES = 32
ROWS = 192
RING = 4
SHARE = D // RING
GROUP = 48
EXP_SCALE = 1.4426950408889634 * SIZE ** -0.5
POS = ("y", "core")
BF16 = jnp.bfloat16
F32 = jnp.float32
VMEM = pl.BlockSpec(memory_space=pltpu.VMEM)
SMEM = pl.BlockSpec(memory_space=pltpu.SMEM)
ANY = pl.BlockSpec(memory_space=pl.ANY)


def shape(*dims, dtype=BF16):
    return jax.ShapeDtypeStruct(dims, dtype)


def params():
    return pltpu.CompilerParams(vmem_limit_bytes=56 * 1024 * 1024)


def cost(flops, nbytes, exps=0):
    return pl.CostEstimate(flops=flops, bytes_accessed=nbytes, transcendentals=exps)


def pack_kernel(ids, place, qkv, *outs):
    y, core = place[0], place[1]
    for part in range(2):
        for step in range(RING):
            to = ((y + step) % RING) * 2 + (core + part) % 2
            for head in range(2):
                column = pl.multiple_of(ids[to * 2 + head] * SIZE, SIZE)
                outs[part * RING + step][:, head] = qkv[:, :, pl.ds(column, SIZE)]
    temporal = outs[8]
    for head in range(HEADS - SPATIAL):
        column = pl.multiple_of(ids[SPATIAL + head] * SIZE, SIZE)
        for piece in range(ROWS // GROUP):
            rows = slice(piece * GROUP, (piece + 1) * GROUP)
            temporal[head * 4 + piece] = qkv[:, rows, pl.ds(column, SIZE)]


def pack(ids, place, qkv):
    outs = [shape(3, 2, ROWS, SIZE)] * 8 + [shape(FRAMES, 3, GROUP, SIZE)]
    return pl.pallas_call(
        pack_kernel,
        out_shape=outs,
        in_specs=[SMEM, SMEM, VMEM],
        out_specs=[VMEM] * 9,
        compiler_params=params(),
        cost_estimate=cost(0, 7_000_000),
        name="pack",
    )(ids, place, qkv)


def attend(query, key, value_ones, keep=None):
    score = lax.dot_general(query, key, (((1,), (1,)), ((), ())), preferred_element_type=F32)
    if keep is not None:
        score = jnp.where(keep, score, -1e30)
    top = jnp.max(score, axis=1, keepdims=True)
    weight = jnp.exp2((score - top) * EXP_SCALE).astype(BF16)
    both = jnp.dot(weight, value_ones, preferred_element_type=F32)
    return (both[:, :SIZE] / both[:, SIZE:]).astype(BF16)


def spatial_kernel(place, *refs):
    chunks, outs = refs[:8], refs[8:]
    y = place[0]
    ones = jnp.ones((8 * ROWS, SIZE), BF16)
    for head in range(2):
        key = jnp.concatenate([chunk[1, head] for chunk in chunks], axis=0)
        value = jnp.concatenate([chunk[2, head] for chunk in chunks], axis=0)
        value_ones = jnp.concatenate([value, ones], axis=1)
        for pair in range(4):
            two = (pair * 2, pair * 2 + 1)
            query = jnp.concatenate([chunks[i][0, head] for i in two], axis=0)
            result = attend(query, key, value_ones)
            for n, i in enumerate(two):
                origin = (y + RING - i % RING) % RING
                outs[i // RING][origin, :, head * SIZE : (head + 1) * SIZE] = result[
                    n * ROWS : (n + 1) * ROWS
                ]


def spatial(place, chunks):
    return pl.pallas_call(
        spatial_kernel,
        out_shape=[shape(RING, ROWS, 2 * SIZE)] * 2,
        in_specs=[SMEM] + [VMEM] * 8,
        out_specs=[VMEM] * 2,
        compiler_params=params(),
        cost_estimate=cost(4_800_000_000, 4_000_000, 4_700_000),
        name="spatial",
    )(place, *chunks)


def temporal_kernel(heads, out):
    span = 16
    count = FRAMES * span
    same = lax.broadcasted_iota(jnp.int32, (count, count), 0) % span == (
        lax.broadcasted_iota(jnp.int32, (count, count), 1) % span
    )
    ones = jnp.ones((count, SIZE), BF16)
    for piece in range(GROUP // span):
        rows = slice(piece * span, (piece + 1) * span)
        query, key, value = (heads[:, c, rows].reshape(count, SIZE) for c in range(3))
        result = attend(query, key, jnp.concatenate([value, ones], axis=1), same)
        out[:, rows] = result.reshape(FRAMES, span, SIZE)


def temporal(heads):
    return pl.pallas_call(
        temporal_kernel,
        out_shape=shape(FRAMES, GROUP, SIZE),
        in_specs=[VMEM],
        out_specs=VMEM,
        compiler_params=params(),
        cost_estimate=cost(600_000_000, 1_600_000, 800_000),
        name="temporal",
    )(heads)


def project_kernel(ids, place, weight, *refs):
    spatial_in = refs[:8]
    temporal_in = (refs[8], refs[9], None, refs[12])
    out, held, tokens, sems = refs[13:]
    y, core = place[0], place[1]
    copies = []
    ranks = []
    for step in range(RING):
        origin = (y + RING - step) % RING
        for part in range(2):
            first = origin * 4 + ((core + part) % 2) * 2
            ranks += [first, first + 1]
    ranks += [SPATIAL + head for head in range(HEADS - SPATIAL)]
    for slot, rank in enumerate(ranks):
        start = pl.multiple_of(ids[rank] * SIZE, SIZE)
        copy = pltpu.make_async_copy(
            weight.at[pl.ds(start, SIZE)], held.at[pl.ds(slot * SIZE, SIZE)], sems.at[slot]
        )
        copy.start()
        copies.append(copy)
    for slot, block in enumerate(spatial_in):
        tokens[:, :, slot * 256 : (slot + 1) * 256] = block[...]
    for step in range(RING):
        origin = (y + RING - step) % RING
        for head in range(HEADS - SPATIAL):
            if step == 2:
                half = (refs[10], refs[11])[head // 4]
                rows = half[(head % 4) * 4 : (head % 4) * 4 + 4]
            else:
                whole = temporal_in[step]
                rows = whole[head * 4 : head * 4 + 4]
            lanes = slice((SPATIAL + head) * SIZE, (SPATIAL + head + 1) * SIZE)
            tokens[origin, :, lanes] = rows.reshape(ROWS, SIZE)
    for copy in copies:
        copy.wait()
    left = tokens[...].reshape(RING * ROWS, D)
    for n in range(SHARE // 256):
        columns = slice(n * 256, (n + 1) * 256)
        total = jnp.dot(left, held[:, columns], preferred_element_type=F32)
        out[:, :, columns] = total.astype(BF16).reshape(RING, ROWS, 256)


def project(ids, place, weight, spatial_in, temporal_in):
    return pl.pallas_call(
        project_kernel,
        out_shape=shape(RING, ROWS, SHARE),
        in_specs=[SMEM, SMEM, ANY] + [VMEM] * 13,
        out_specs=VMEM,
        scratch_shapes=[
            pltpu.VMEM((D, SHARE), BF16),
            pltpu.VMEM((RING, ROWS, D), BF16),
            pltpu.SemaphoreType.DMA((HEADS,)),
        ],
        compiler_params=params(),
        cost_estimate=cost(3_600_000_000, 11_000_000),
        name="project",
    )(ids, place, weight, *spatial_in, *temporal_in)


def hop(array, steps, part=0):
    perm = [
        (y * 2 + core, ((y + steps) % RING) * 2 + (core + part) % 2)
        for y in range(RING)
        for core in range(2)
    ]
    return lax.ppermute(array, POS, perm)


def weight_share(out_weight):
    here = jnp.transpose(out_weight.reshape(12, RING, SHARE), (1, 0, 2))
    sent = jnp.broadcast_to(here[:, None], (RING, 2, 12, SHARE)).reshape(8, 12, SHARE)
    rows = lax.all_to_all(sent, POS, 0, 0, tiled=True).reshape(96, SHARE)
    own = lax.dynamic_slice_in_dim(rows, lax.axis_index("core") * 48, 48, 0)
    gathered = lax.all_gather(own, ("frame", "core"), axis=0, tiled=False)
    return gathered.reshape(D, SHARE)


def shards(qkv, head_kind, out_weight):
    y = lax.axis_index("y")
    core = lax.axis_index("core")
    place = jnp.stack([y, core]).astype(jnp.int32)
    ids = jnp.argsort(head_kind, stable=True).astype(jnp.int32)
    weight = weight_share(out_weight)

    packed = pack(ids, place, qkv.reshape(3, ROWS, D))
    chunks = [packed[0]]
    for i in range(1, 8):
        chunks.append(hop(packed[i], i % RING, i // RING))
    across = lax.all_to_all(packed[8], "frame", 0, 0, tiled=True)
    mine, other = spatial(place, chunks)
    theirs = hop(other, 0, 1)
    mine_behind, mine_ahead = hop(mine, 1), hop(mine, -1)
    theirs_behind, theirs_ahead = hop(theirs, 1), hop(theirs, -1)
    mine_far = hop(mine_behind, 1)
    theirs_far = hop(theirs_ahead, -1)

    back = lax.all_to_all(temporal(across), "frame", 0, 0, tiled=True)
    back_behind, back_ahead = hop(back, 1), hop(back, -1)
    far_low = hop(back_behind[:16], 1)
    far_high = hop(back_ahead[16:], -1)

    out = project(
        ids,
        place,
        weight,
        [mine, theirs, mine_behind, theirs_behind, mine_far, theirs_far, mine_ahead, theirs_ahead],
        [back, back_behind, far_low, far_high, back_ahead],
    )
    whole = lax.all_to_all(out, "y", 0, 0, tiled=True)
    return jnp.transpose(whole, (1, 0, 2)).reshape(1, ROWS, D)


def solution(mesh):
    frames, positions = mesh.devices.shape
    split = Mesh(
        mesh.devices.reshape(frames, positions // 2, 2), ("frame", "y", "core")
    )
    placed = (P(None, "frame", POS, None), P(), P(("frame", "y", "core"), None))
    return jax.shard_map(
        shards, mesh=split, in_specs=placed, out_specs=P("frame", POS, None), check_vma=False
    )
```

```python
import jax
import jax.numpy as jnp
from jax import lax
from jax.experimental import pallas as pl
from jax.experimental.pallas import tpu as pltpu
from jax.sharding import Mesh, PartitionSpec as P

HEADS = 24
SIZE = 128
SPATIAL = 16
D = 3072
FRAMES = 32
ROWS = 192
RING = 4
SHARE = D // RING
GROUP = 48
EXP_SCALE = 1.4426950408889634 * SIZE ** -0.5
POS = ("y", "core")
BF16 = jnp.bfloat16
F32 = jnp.float32
VMEM = pl.BlockSpec(memory_space=pltpu.VMEM)
SMEM = pl.BlockSpec(memory_space=pltpu.SMEM)
ANY = pl.BlockSpec(memory_space=pl.ANY)


def shape(*dims, dtype=BF16):
    return jax.ShapeDtypeStruct(dims, dtype)


def params():
    return pltpu.CompilerParams(vmem_limit_bytes=56 * 1024 * 1024)


def cost(flops, nbytes, exps=0):
    return pl.CostEstimate(flops=flops, bytes_accessed=nbytes, transcendentals=exps)


def rank_heads(kinds, ids):
    spatial_next, temporal_next = jnp.int32(0), jnp.int32(SPATIAL)
    for head in range(HEADS):
        kind = kinds[head]
        ids[jnp.where(kind == 0, spatial_next, temporal_next)] = head
        spatial_next, temporal_next = spatial_next + 1 - kind, temporal_next + kind


def head_columns(ids, rank):
    return pl.ds(pl.multiple_of(ids[rank] * SIZE, SIZE), SIZE)


def run_copies(pairs, sems):
    copies = [pltpu.make_async_copy(a, b, sems.at[i]) for i, (a, b) in enumerate(pairs)]
    for copy in copies:
        copy.start()
    return copies


def pack_temporal_kernel(kinds, qkv, out, ids, sems):
    rank_heads(kinds, ids)
    pairs = []
    for head in range(HEADS - SPATIAL):
        columns = head_columns(ids, SPATIAL + head)
        for piece in range(RING):
            rows = pl.ds(piece * GROUP, GROUP)
            pairs.append((qkv.at[:, rows, columns], out.at[head * RING + piece]))
    for copy in run_copies(pairs, sems):
        copy.wait()


def pack_temporal(kinds, qkv):
    return pl.pallas_call(
        pack_temporal_kernel,
        out_shape=shape(FRAMES, 3, GROUP, SIZE),
        in_specs=[SMEM, ANY],
        out_specs=ANY,
        scratch_shapes=[pltpu.SMEM((HEADS,), jnp.int32), pltpu.SemaphoreType.DMA((FRAMES,))],
        compiler_params=params(),
        cost_estimate=cost(0, 2_400_000),
        name="pack_temporal",
    )(kinds, qkv)


def pack_spatial_kernel(kinds, qkv, *refs):
    outs, (ids, sems) = refs[:8], refs[8:]
    rank_heads(kinds, ids)
    y, core = lax.axis_index("y"), lax.axis_index("core")
    pairs = []
    for part in range(2):
        for step in range(RING):
            to = lax.rem(y + step, RING) * 2 + lax.rem(core + part, 2)
            for head in range(2):
                columns = head_columns(ids, to * 2 + head)
                pairs.append((qkv.at[:, :, columns], outs[part * RING + step].at[:, head]))
    for copy in run_copies(pairs, sems):
        copy.wait()


def pack_spatial(kinds, qkv):
    return pl.pallas_call(
        pack_spatial_kernel,
        out_shape=[shape(3, 2, ROWS, SIZE)] * 8,
        in_specs=[SMEM, ANY],
        out_specs=[ANY] * 8,
        scratch_shapes=[pltpu.SMEM((HEADS,), jnp.int32), pltpu.SemaphoreType.DMA((16,))],
        compiler_params=params(),
        cost_estimate=cost(0, 4_800_000),
        name="pack_spatial",
    )(kinds, qkv)


def attend(query, key, value_ones, keep=None):
    score = lax.dot_general(query, key, (((1,), (1,)), ((), ())), preferred_element_type=F32)
    if keep is not None:
        score = jnp.where(keep, score, -1e30)
    top = jnp.max(score, axis=1, keepdims=True)
    weight = jnp.exp2((score - top) * EXP_SCALE).astype(BF16)
    both = jnp.dot(weight, value_ones, preferred_element_type=F32)
    return (both[:, :SIZE] / both[:, SIZE:]).astype(BF16)


def spatial_kernel(*refs):
    chunks, outs = refs[:8], refs[8:]
    y = lax.axis_index("y")
    ones = jnp.ones((8 * ROWS, SIZE), BF16)
    for head in range(2):
        key = jnp.concatenate([chunk[1, head] for chunk in chunks], axis=0)
        value = jnp.concatenate([chunk[2, head] for chunk in chunks], axis=0)
        value_ones = jnp.concatenate([value, ones], axis=1)
        for pair in range(4):
            two = (pair * 2, pair * 2 + 1)
            query = jnp.concatenate([chunks[i][0, head] for i in two], axis=0)
            result = attend(query, key, value_ones)
            for n, i in enumerate(two):
                origin = lax.rem(y + RING - i % RING, RING)
                outs[i // RING][origin, :, head * SIZE : (head + 1) * SIZE] = result[
                    n * ROWS : (n + 1) * ROWS
                ]


def spatial(chunks):
    return pl.pallas_call(
        spatial_kernel,
        out_shape=[shape(RING, ROWS, 2 * SIZE)] * 2,
        in_specs=[VMEM] * 8,
        out_specs=[VMEM] * 2,
        compiler_params=params(),
        cost_estimate=cost(4_800_000_000, 4_000_000, 4_700_000),
        name="spatial",
    )(*chunks)


def temporal_kernel(heads, out):
    span = 16
    count = FRAMES * span
    same = lax.broadcasted_iota(jnp.int32, (count, count), 0) % span == (
        lax.broadcasted_iota(jnp.int32, (count, count), 1) % span
    )
    ones = jnp.ones((count, SIZE), BF16)
    for piece in range(GROUP // span):
        rows = slice(piece * span, (piece + 1) * span)
        query, key, value = (heads[:, c, rows].reshape(count, SIZE) for c in range(3))
        result = attend(query, key, jnp.concatenate([value, ones], axis=1), same)
        out[:, rows] = result.reshape(FRAMES, span, SIZE)


def temporal(heads):
    return pl.pallas_call(
        temporal_kernel,
        out_shape=shape(FRAMES, GROUP, SIZE),
        in_specs=[VMEM],
        out_specs=VMEM,
        compiler_params=params(),
        cost_estimate=cost(600_000_000, 1_600_000, 800_000),
        name="temporal",
    )(heads)


def arrange_kernel(own, behind, ahead, far_low, far_high, out, sems):
    z, x = lax.axis_index("z"), lax.axis_index("x")
    pairs = []
    for step, halves in enumerate(
        ((own.at[:4], own.at[4:]), (behind.at[:4], behind.at[4:]), (far_low, far_high), (ahead.at[:4], ahead.at[4:]))
    ):
        x_from = lax.rem(x + RING - step, RING)
        for slab in range(8):
            z_from = lax.rem(z + 8 - slab, 8)
            pairs.append((halves[slab // 4].at[slab % 4], out.at[z_from * 4 + x_from]))
    for copy in run_copies(pairs, sems):
        copy.wait()


def arrange(*blocks):
    return pl.pallas_call(
        arrange_kernel,
        out_shape=shape(FRAMES, 96, SHARE // 2),
        in_specs=[ANY] * 5,
        out_specs=ANY,
        scratch_shapes=[pltpu.SemaphoreType.DMA((FRAMES,))],
        compiler_params=params(),
        cost_estimate=cost(0, 4_800_000),
        name="arrange",
    )(*blocks)


def weight_pairs(ids, ranks, halves, target):
    core = lax.axis_index("core")
    pairs = []
    for slot, rank in enumerate(ranks):
        rows = head_columns(ids, rank)
        for part, half in enumerate(halves):
            start = pl.multiple_of(lax.rem(core + part, 2) * (SHARE // 2), SIZE)
            to = target.at[pl.ds(slot * SIZE, SIZE), pl.ds(start, SHARE // 2)]
            pairs.append((half.at[rows], to))
    return pairs


def project_spatial_kernel(kinds, weight_own, weight_other, *refs):
    blocks = refs[:8]
    total, weight_temporal, ids, held, tokens, sems = refs[8:]
    y, core = lax.axis_index("y"), lax.axis_index("core")
    rank_heads(kinds, ids)
    ranks = []
    for step in range(RING):
        origin = lax.rem(y + RING - step, RING)
        for part in range(2):
            first = origin * 4 + lax.rem(core + part, 2) * 2
            ranks += [first, first + 1]
    halves = (weight_own, weight_other)
    pairs = weight_pairs(ids, ranks, halves, held)
    pairs += weight_pairs(ids, range(SPATIAL, HEADS), halves, weight_temporal)
    copies = run_copies(pairs, sems)
    for slot, block in enumerate(blocks):
        tokens[:, :, slot * 256 : (slot + 1) * 256] = block[...]
    for copy in copies:
        copy.wait()
    left = tokens[...].reshape(RING * ROWS, SPATIAL * SIZE)
    for n in range(SHARE // 256):
        columns = slice(n * 256, (n + 1) * 256)
        product = jnp.dot(left, held[:, columns], preferred_element_type=F32)
        total[:, :, columns] = product.reshape(RING, ROWS, 256)


def project_spatial(kinds, weight_own, weight_other, blocks):
    return pl.pallas_call(
        project_spatial_kernel,
        out_shape=[shape(RING, ROWS, SHARE, dtype=F32), shape(D - SPATIAL * SIZE, SHARE)],
        in_specs=[SMEM, ANY, ANY] + [VMEM] * 8,
        out_specs=[VMEM, ANY],
        scratch_shapes=[
            pltpu.SMEM((HEADS,), jnp.int32),
            pltpu.VMEM((SPATIAL * SIZE, SHARE), BF16),
            pltpu.VMEM((RING, ROWS, SPATIAL * SIZE), BF16),
            pltpu.SemaphoreType.DMA((2 * HEADS,)),
        ],
        compiler_params=params(),
        cost_estimate=cost(2_400_000_000, 11_000_000),
        name="project_spatial",
    )(kinds, weight_own, weight_other, *blocks)


def project_temporal(total, weight, halves, steps, pieces):
    count = len(steps)

    def kernel(total, weight, *refs):
        ins, outs, held, sems = refs[: 2 * count], refs[2 * count : -2], refs[-2], refs[-1]
        y = lax.axis_index("y")
        pairs = [
            (total.at[lax.rem(y + RING - step, RING)], held.at[i]) for i, step in enumerate(steps)
        ]
        copies = run_copies(pairs, sems)
        lefts = []
        for i in range(count):
            heads = []
            for half in ins[2 * i : 2 * i + 2]:
                heads += [half[h * 4 : h * 4 + 4].reshape(ROWS, SIZE) for h in range(4)]
            lefts.append(jnp.concatenate(heads, axis=1))
        left = jnp.concatenate(lefts, axis=0)
        for copy in copies:
            copy.wait()
        rows = ROWS // pieces
        for n in range(SHARE // 256):
            columns = slice(n * 256, (n + 1) * 256)
            product = jnp.dot(left, weight[:, columns], preferred_element_type=F32)
            for i in range(count):
                whole = held[i, :, columns] + product[i * ROWS : (i + 1) * ROWS]
                for piece in range(pieces):
                    outs[i * pieces + piece][:, columns] = whole[
                        piece * rows : (piece + 1) * rows
                    ].astype(BF16)

    return pl.pallas_call(
        kernel,
        out_shape=[shape(ROWS // pieces, SHARE)] * (count * pieces),
        in_specs=[ANY] + [VMEM] * (2 * count + 1),
        out_specs=[VMEM] * (count * pieces),
        scratch_shapes=[
            pltpu.VMEM((count, ROWS, SHARE), F32),
            pltpu.SemaphoreType.DMA((count,)),
        ],
        compiler_params=params(),
        cost_estimate=cost(300_000_000 * count, 2_000_000 + 1_300_000 * count),
        name="project_temporal",
    )(total, weight, *[half for pair in halves for half in pair])


def finish_kernel(own, behind, ahead, far_low, far_high, out, sems):
    y = lax.axis_index("y")
    half = ROWS // 2

    def columns(step):
        return pl.ds(pl.multiple_of(lax.rem(y + RING - step, RING) * SHARE, SIZE), SHARE)

    pairs = [
        (own, out.at[:, columns(0)]),
        (behind, out.at[:, columns(1)]),
        (far_low, out.at[:half, columns(2)]),
        (far_high, out.at[half:, columns(2)]),
        (ahead, out.at[:, columns(3)]),
    ]
    for copy in run_copies(pairs, sems):
        copy.wait()


def finish(*blocks):
    return pl.pallas_call(
        finish_kernel,
        out_shape=shape(ROWS, D),
        in_specs=[ANY] * 5,
        out_specs=ANY,
        scratch_shapes=[pltpu.SemaphoreType.DMA((5,))],
        compiler_params=params(),
        cost_estimate=cost(0, 2_400_000),
        name="finish",
    )(*blocks)


def hop(array, axis, steps):
    size = lax.axis_size(axis)
    return lax.ppermute(array, axis, [(i, (i + steps) % size) for i in range(size)])


def hop_over(array, steps):
    perm = [
        (y * 2 + core, ((y + steps) % RING) * 2 + 1 - core)
        for y in range(RING)
        for core in range(2)
    ]
    return lax.ppermute(array, POS, perm)


def weight_halves(out_weight):
    sent = jnp.transpose(out_weight.reshape(12, 8, SHARE // 2), (1, 0, 2))
    slab = lax.all_to_all(sent, POS, 0, 0, tiled=True).reshape(96, SHARE // 2)
    forward, backward = [slab], []
    for _ in range(4):
        forward.append(hop(forward[-1], "z", 1))
    for _ in range(3):
        backward.append(hop(backward[-1] if backward else slab, "z", -1))
    slabs = jnp.stack(forward + backward[::-1])
    behind, ahead = hop(slabs, "x", 1), hop(slabs, "x", -1)
    far_low, far_high = hop(behind[:4], "x", 1), hop(ahead[4:], "x", -1)
    own = arrange(slabs, behind, ahead, far_low, far_high).reshape(D, SHARE // 2)
    return own, hop(own, "core", 1)


def shards(qkv, head_kind, out_weight):
    qkv = qkv.reshape(3, ROWS, D)
    across = lax.all_to_all(pack_temporal(head_kind, qkv), ("z", "x"), 0, 0, tiled=True)

    packed = pack_spatial(head_kind, qkv)
    far_same = hop(packed[2], "y", 1)
    far_cross = hop(packed[6], "y", -1)
    chunks = [
        packed[0],
        hop(packed[1], "y", 1),
        hop(far_same, "y", 1),
        hop(packed[3], "y", -1),
        hop(packed[4], "core", 1),
        hop_over(packed[5], 1),
        hop_over(far_cross, -1),
        hop_over(packed[7], -1),
    ]
    weight_own, weight_other = weight_halves(out_weight)

    mine, other = spatial(chunks)
    theirs = hop(other, "core", 1)
    mine_behind, mine_ahead = hop(mine, "y", 1), hop(mine, "y", -1)
    theirs_behind, theirs_ahead = hop(theirs, "y", 1), hop(theirs, "y", -1)
    mine_far = hop(mine_behind, "y", 1)
    theirs_far = hop(theirs_ahead, "y", -1)

    back = lax.all_to_all(temporal(across), ("z", "x"), 0, 0, tiled=True)
    low, high = back[:16], back[16:]
    low_behind, high_ahead = hop(low, "y", 1), hop(high, "y", -1)
    high_behind, low_ahead = hop(high, "y", 1), hop(low, "y", -1)
    low_far, high_far = hop(low_behind, "y", 1), hop(high_ahead, "y", -1)

    blocks = [mine, theirs, mine_behind, theirs_behind, mine_far, theirs_far, mine_ahead, theirs_ahead]
    total, weight_temporal = project_spatial(head_kind, weight_own, weight_other, blocks)
    out_far = project_temporal(total, weight_temporal, [(low_far, high_far)], [2], 2)
    out_behind, out_ahead = project_temporal(
        total,
        weight_temporal,
        [(low_behind, high_behind), (low_ahead, high_ahead)],
        [1, 3],
        1,
    )
    (out_own,) = project_temporal(total, weight_temporal, [(low, high)], [0], 1)
    from_far_low = hop(hop(out_far[0], "y", 1), "y", 1)
    from_far_high = hop(hop(out_far[1], "y", -1), "y", -1)
    from_behind, from_ahead = hop(out_ahead, "y", 1), hop(out_behind, "y", -1)
    whole = finish(out_own, from_behind, from_ahead, from_far_low, from_far_high)
    return whole.reshape(1, ROWS, D)


def solution(mesh):
    split = Mesh(mesh.devices.reshape(8, 4, 4, 2), ("z", "x", "y", "core"))
    placed = (P(None, ("z", "x"), POS, None), P(), P(("z", "x", "y", "core"), None))
    return jax.shard_map(
        shards, mesh=split, in_specs=placed, out_specs=P(("z", "x"), POS, None), check_vma=False
    )
```

```python
import jax
import jax.numpy as jnp
from jax import lax
from jax.experimental import pallas as pl
from jax.experimental.pallas import tpu as pltpu
from jax.sharding import Mesh, PartitionSpec as P

HEADS = 24
SIZE = 128
SPATIAL = 16
D = 3072
FRAMES = 32
ROWS = 192
RING = 4
SHARE = D // RING
GROUP = 48
EXP_SCALE = 1.4426950408889634 * SIZE ** -0.5
POS = ("y", "core")
BF16 = jnp.bfloat16
F32 = jnp.float32
SPATIAL_COST = 4_800_000_000
HALVE_COST = 40_000_000_000
COLLECT_COST = 40_000_000_000
VMEM = pl.BlockSpec(memory_space=pltpu.VMEM)
SMEM = pl.BlockSpec(memory_space=pltpu.SMEM)
ANY = pl.BlockSpec(memory_space=pl.ANY)


def shape(*dims, dtype=BF16):
    return jax.ShapeDtypeStruct(dims, dtype)


def params(mebibytes):
    return pltpu.CompilerParams(vmem_limit_bytes=mebibytes * 1024 * 1024)


def cost(flops, nbytes, exps=0):
    return pl.CostEstimate(flops=flops, bytes_accessed=nbytes, transcendentals=exps)


def rank_heads(kinds, ids):
    spatial_next, temporal_next = jnp.int32(0), jnp.int32(SPATIAL)
    for head in range(HEADS):
        kind = kinds[head]
        ids[jnp.where(kind == 0, spatial_next, temporal_next)] = head
        spatial_next, temporal_next = spatial_next + 1 - kind, temporal_next + kind


def head_columns(ids, rank):
    return pl.ds(pl.multiple_of(ids[rank] * SIZE, SIZE), SIZE)


def pack_spatial_kernel(kinds, qkv, *refs):
    outs, ids = refs[:8], refs[8]

    @pl.when(pl.program_id(0) == 0)
    def _():
        rank_heads(kinds, ids)

    y, core = lax.axis_index("y"), lax.axis_index("core")
    for part in range(2):
        for step in range(RING):
            to = lax.rem(y + step, RING) * 2 + lax.rem(core + part, 2)
            for head in range(2):
                outs[part * RING + step][0, head] = qkv[0, :, head_columns(ids, to * 2 + head)]


def pack_temporal_kernel(kinds, qkv, out, ids):
    @pl.when(pl.program_id(0) == 0)
    def _():
        rank_heads(kinds, ids)

    for head in range(HEADS - SPATIAL):
        columns = head_columns(ids, SPATIAL + head)
        for piece in range(RING):
            rows = slice(piece * GROUP, (piece + 1) * GROUP)
            out[head * RING + piece, 0] = qkv[0, rows, columns]


def pack_call(kernel, name, block, count):
    spec = pl.BlockSpec(
        (block[0], 1) + block[2:] if name == "pack_temporal" else (1,) + block[1:],
        (lambda c: (0, c, 0, 0)) if name == "pack_temporal" else (lambda c: (c, 0, 0, 0)),
    )
    return pl.pallas_call(
        kernel,
        grid=(3,),
        out_shape=[shape(*block)] * count,
        in_specs=[SMEM, pl.BlockSpec((1, ROWS, D), lambda c: (c, 0, 0))],
        out_specs=[spec] * count,
        scratch_shapes=[pltpu.SMEM((HEADS,), jnp.int32)],
        compiler_params=params(56),
        cost_estimate=cost(0, 4_800_000),
        name=name,
    )


def pack_spatial(kinds, qkv):
    return pack_call(pack_spatial_kernel, "pack_spatial", (3, 2, ROWS, SIZE), 8)(kinds, qkv)


def pack_temporal(kinds, qkv):
    return pack_call(pack_temporal_kernel, "pack_temporal", (FRAMES, 3, GROUP, SIZE), 1)(kinds, qkv)[0]


def attend(query, key, value_ones, keep=None):
    score = lax.dot_general(query, key, (((1,), (1,)), ((), ())), preferred_element_type=F32)
    if keep is not None:
        score = jnp.where(keep, score, -1e30)
    top = jnp.max(score, axis=1, keepdims=True)
    weight = jnp.exp2((score - top) * EXP_SCALE).astype(BF16)
    both = jnp.dot(weight, value_ones, preferred_element_type=F32)
    return (both[:, :SIZE] / both[:, SIZE:]).astype(BF16)


def spatial_kernel(*refs):
    chunks, outs = refs[:8], refs[8:]
    y = lax.axis_index("y")
    ones = jnp.ones((8 * ROWS, SIZE), BF16)
    for head in range(2):
        key = jnp.concatenate([chunk[1, head] for chunk in chunks], axis=0)
        value = jnp.concatenate([chunk[2, head] for chunk in chunks], axis=0)
        value_ones = jnp.concatenate([value, ones], axis=1)
        for pair in range(4):
            two = (pair * 2, pair * 2 + 1)
            query = jnp.concatenate([chunks[i][0, head] for i in two], axis=0)
            result = attend(query, key, value_ones)
            for n, i in enumerate(two):
                origin = lax.rem(y + RING - i % RING, RING)
                outs[i // RING][origin, :, head * SIZE : (head + 1) * SIZE] = result[
                    n * ROWS : (n + 1) * ROWS
                ]


def spatial(chunks):
    return pl.pallas_call(
        spatial_kernel,
        out_shape=[shape(RING, ROWS, 2 * SIZE)] * 2,
        in_specs=[VMEM] * 8,
        out_specs=[VMEM] * 2,
        compiler_params=params(24),
        cost_estimate=cost(SPATIAL_COST, 4_000_000, 4_700_000),
        name="spatial",
    )(*chunks)


def temporal_kernel(heads, _, out):
    span = 16
    count = FRAMES * span
    same = lax.broadcasted_iota(jnp.int32, (count, count), 0) % span == (
        lax.broadcasted_iota(jnp.int32, (count, count), 1) % span
    )
    ones = jnp.ones((count, SIZE), BF16)
    for piece in range(GROUP // span):
        rows = slice(piece * span, (piece + 1) * span)
        query, key, value = (heads[:, c, rows].reshape(count, SIZE) for c in range(3))
        result = attend(query, key, jnp.concatenate([value, ones], axis=1), same)
        out[:, rows] = result.reshape(FRAMES, span, SIZE)


def temporal(heads, done):
    return pl.pallas_call(
        temporal_kernel,
        out_shape=shape(FRAMES, GROUP, SIZE),
        in_specs=[VMEM, ANY],
        out_specs=VMEM,
        compiler_params=params(16),
        cost_estimate=cost(600_000_000, 1_600_000, 800_000),
        name="temporal",
    )(heads, done)


def after(arrays, done):
    def kernel(*refs):
        for i in range(len(arrays)):
            refs[len(arrays) + 1 + i][...] = refs[i][...]

    return pl.pallas_call(
        kernel,
        out_shape=[shape(*array.shape) for array in arrays],
        in_specs=[VMEM] * len(arrays) + [ANY],
        out_specs=[VMEM] * len(arrays),
        compiler_params=params(4),
        cost_estimate=cost(0, 300_000),
        name="after",
    )(*arrays, done)


def join3_kernel(first, second, third, _, out):
    for i, ref in enumerate((first, second, third)):
        out[i] = ref[...]


def join3(slabs, done):
    return pl.pallas_call(
        join3_kernel,
        out_shape=shape(3, *slabs[0].shape),
        in_specs=[VMEM] * 3 + [ANY],
        out_specs=VMEM,
        compiler_params=params(4),
        cost_estimate=cost(0, 400_000),
        name="join3",
    )(*slabs, done)


def join8_kernel(near, behind, ahead, _, out):
    z = lax.axis_index("z")
    for i in range(3):
        out[lax.rem(z + 7 + i, 8)] = near[i]
        out[lax.rem(z + 4 + i, 8)] = behind[i]
    for i in range(2):
        out[lax.rem(z + 2 + i, 8)] = ahead[i]


def join8(near, behind, ahead, done):
    return pl.pallas_call(
        join8_kernel,
        out_shape=shape(8, *near.shape[1:]),
        in_specs=[VMEM] * 3 + [ANY],
        out_specs=VMEM,
        compiler_params=params(4),
        cost_estimate=cost(0, 1_200_000),
        name="join8",
    )(near, behind, ahead, done)


def arrange_kernel(own, behind, far, ahead, out):
    x = lax.axis_index("x")
    for step, block in enumerate((own, behind, far, ahead)):
        x_from = lax.rem(x + RING - step, RING)
        for z in range(8):
            out[z * RING + x_from] = block[z]


def arrange(*blocks):
    return pl.pallas_call(
        arrange_kernel,
        out_shape=shape(FRAMES, 96, SHARE // 2),
        in_specs=[VMEM] * 4,
        out_specs=VMEM,
        compiler_params=params(12),
        cost_estimate=cost(0, 4_800_000),
        name="arrange",
    )(*blocks)


def halve_kernel(whole, low, high):
    low[...] = whole[:16]
    high[...] = whole[16:]


def halve(whole):
    return pl.pallas_call(
        halve_kernel,
        out_shape=[shape(16, GROUP, SIZE)] * 2,
        in_specs=[VMEM],
        out_specs=[VMEM] * 2,
        compiler_params=params(4),
        cost_estimate=cost(HALVE_COST, 800_000),
        name="halve",
    )(whole)


def collect_kernel(*refs):
    for slot in range(8):
        refs[8][:, :, slot * 256 : (slot + 1) * 256] = refs[slot][...]


def collect(blocks):
    return pl.pallas_call(
        collect_kernel,
        out_shape=shape(RING, ROWS, SPATIAL * SIZE),
        in_specs=[VMEM] * 8,
        out_specs=VMEM,
        compiler_params=params(12),
        cost_estimate=cost(COLLECT_COST, 6_400_000),
        name="collect",
    )(*blocks)


def project_spatial_kernel(kinds, weight_own, weight_other, tokens, total, weight_temporal, ids, held):
    y, core = lax.axis_index("y"), lax.axis_index("core")
    rank_heads(kinds, ids)
    ranks = []
    for step in range(RING):
        origin = lax.rem(y + RING - step, RING)
        for part in range(2):
            first = origin * 4 + lax.rem(core + part, 2) * 2
            ranks += [first, first + 1]
    left = tokens[...].reshape(RING * ROWS, SPATIAL * SIZE)
    for part, half in enumerate((weight_own, weight_other)):
        start = pl.multiple_of(lax.rem(core + part, 2) * (SHARE // 2), SIZE)
        columns = pl.ds(start, SHARE // 2)
        for slot, rank in enumerate(ranks):
            held[slot * SIZE : (slot + 1) * SIZE] = half[head_columns(ids, rank)]
        for head in range(HEADS - SPATIAL):
            rows = slice(head * SIZE, (head + 1) * SIZE)
            weight_temporal[rows, columns] = half[head_columns(ids, SPATIAL + head)]
        product = jnp.dot(left, held[...], preferred_element_type=F32)
        total[:, :, columns] = product.reshape(RING, ROWS, SHARE // 2)


def project_spatial(kinds, weight_own, weight_other, tokens):
    return pl.pallas_call(
        project_spatial_kernel,
        out_shape=[shape(RING, ROWS, SHARE, dtype=F32), shape(D - SPATIAL * SIZE, SHARE)],
        in_specs=[SMEM] + [VMEM] * 3,
        out_specs=[VMEM, VMEM],
        scratch_shapes=[
            pltpu.SMEM((HEADS,), jnp.int32),
            pltpu.VMEM((SPATIAL * SIZE, SHARE // 2), BF16),
        ],
        compiler_params=params(32),
        cost_estimate=cost(2_400_000_000, 11_000_000),
        name="project_spatial",
    )(kinds, weight_own, weight_other, tokens)


def project_temporal_kernel(total, weight, *refs):
    ins, out = refs[:8], refs[8]
    y = lax.axis_index("y")
    for step in range(RING):
        origin = lax.rem(y + RING - step, RING)
        heads = []
        for half in ins[2 * step : 2 * step + 2]:
            heads += [half[h * 4 : h * 4 + 4].reshape(ROWS, SIZE) for h in range(4)]
        left = jnp.concatenate(heads, axis=1)
        product = jnp.dot(left, weight[...], preferred_element_type=F32)
        out[origin] = (total[origin] + product).astype(BF16)


def project_temporal(total, weight, halves):
    return pl.pallas_call(
        project_temporal_kernel,
        out_shape=shape(RING, ROWS, SHARE),
        in_specs=[VMEM] * 10,
        out_specs=VMEM,
        compiler_params=params(24),
        cost_estimate=cost(1_200_000_000, 7_000_000),
        name="project_temporal",
    )(total, weight, *halves)


def finish_kernel(blocks, out):
    for y in range(RING):
        out[:, y * SHARE : (y + 1) * SHARE] = blocks[y]


def finish(blocks):
    return pl.pallas_call(
        finish_kernel,
        out_shape=shape(ROWS, D),
        in_specs=[VMEM],
        out_specs=VMEM,
        compiler_params=params(8),
        cost_estimate=cost(0, 2_400_000),
        name="finish",
    )(blocks)


def hop(array, axis, steps):
    size = lax.axis_size(axis)
    return lax.ppermute(array, axis, [(i, (i + steps) % size) for i in range(size)])


def hop_over(array, steps):
    perm = [
        (y * 2 + core, ((y + steps) % RING) * 2 + 1 - core)
        for y in range(RING)
        for core in range(2)
    ]
    return lax.ppermute(array, POS, perm)


def weight_slab(out_weight):
    sent = jnp.transpose(out_weight.reshape(12, 8, SHARE // 2), (1, 0, 2))
    return lax.all_to_all(sent, POS, 0, 0, tiled=True).reshape(96, SHARE // 2)


def shards(qkv, head_kind, out_weight):
    qkv = qkv.reshape(3, ROWS, D)
    slab = weight_slab(out_weight)
    across = lax.all_to_all(pack_temporal(head_kind, qkv), ("z", "x"), 0, 0, tiled=True)
    packed = pack_spatial(head_kind, qkv)
    far_same, far_cross = hop(packed[2], "y", 1), hop(packed[6], "y", -1)
    chunks = [
        packed[0],
        hop(packed[1], "y", 1),
        hop(far_same, "y", 1),
        hop(packed[3], "y", -1),
        hop(packed[4], "core", 1),
        hop_over(packed[5], 1),
        hop_over(far_cross, -1),
        hop_over(packed[7], -1),
    ]
    (slab,) = after([slab], far_same)
    near = join3([hop(slab, "z", 1), slab, hop(slab, "z", -1)], chunks[2])
    near_behind, near_ahead = hop(near, "z", 3), hop(near, "z", -3)

    mine, other = spatial(chunks)
    theirs = hop(other, "core", 1)
    mine_behind, mine_ahead = hop(mine, "y", 1), hop(mine, "y", -1)
    theirs_behind, theirs_ahead = hop(theirs, "y", 1), hop(theirs, "y", -1)
    mine_far = hop(mine_behind, "y", 1)
    theirs_far = hop(theirs_ahead, "y", -1)

    slabs = join8(near, near_behind, near_ahead, mine)
    w_behind, w_ahead = hop(slabs, "x", 1), hop(slabs, "x", -1)
    w_far = hop(w_behind, "x", 1)
    weight_own = arrange(slabs, w_behind, w_far, w_ahead).reshape(D, SHARE // 2)
    weight_other = hop(weight_own, "core", 1)

    back = lax.all_to_all(temporal(across, mine_behind), ("z", "x"), 0, 0, tiled=True)
    low, high = halve(back)
    low_behind, high_ahead = hop(low, "y", 1), hop(high, "y", -1)
    high_behind, low_ahead = hop(high, "y", 1), hop(low, "y", -1)
    low_far, high_far = hop(low_behind, "y", 1), hop(high_ahead, "y", -1)

    blocks = [mine, theirs, mine_behind, theirs_behind, mine_far, theirs_far, mine_ahead, theirs_ahead]
    total, weight_temporal = project_spatial(head_kind, weight_own, weight_other, collect(blocks))
    halves = [low, high, low_behind, high_behind, low_far, high_far, low_ahead, high_ahead]
    out = project_temporal(total, weight_temporal, halves)
    return finish(lax.all_to_all(out, "y", 0, 0, tiled=True)).reshape(1, ROWS, D)


def solution(mesh):
    split = Mesh(mesh.devices.reshape(8, 4, 4, 2), ("z", "x", "y", "core"))
    placed = (P(None, ("z", "x"), POS, None), P(), P(("z", "x", "y", "core"), None))
    return jax.shard_map(
        shards, mesh=split, in_specs=placed, out_specs=P(("z", "x"), POS, None), check_vma=False
    )
```

```python
import jax
import jax.numpy as jnp
from jax import lax
from jax.experimental import pallas as pl
from jax.experimental.pallas import tpu as pltpu
from jax.sharding import Mesh, PartitionSpec as P

HEADS = 24
SIZE = 128
SPATIAL = 16
D = 3072
FRAMES = 32
ROWS = 192
RING = 4
SHARE = D // RING
GROUP = 48
EXP_SCALE = 1.4426950408889634 * SIZE ** -0.5
POS = ("y", "core")
BF16 = jnp.bfloat16
F32 = jnp.float32
TEMPORAL_COST = 600_000_000
HALVE_COST = 40_000_000_000
COLLECT_COST = 40_000_000_000
VMEM = pl.BlockSpec(memory_space=pltpu.VMEM)
SMEM = pl.BlockSpec(memory_space=pltpu.SMEM)
ANY = pl.BlockSpec(memory_space=pl.ANY)


def shape(*dims, dtype=BF16):
    return jax.ShapeDtypeStruct(dims, dtype)


def params(mebibytes):
    return pltpu.CompilerParams(vmem_limit_bytes=mebibytes * 1024 * 1024)


def cost(flops, nbytes, exps=0):
    return pl.CostEstimate(flops=flops, bytes_accessed=nbytes, transcendentals=exps)


def rank_heads(kinds, ids):
    spatial_next, temporal_next = jnp.int32(0), jnp.int32(SPATIAL)
    for head in range(HEADS):
        kind = kinds[head]
        ids[jnp.where(kind == 0, spatial_next, temporal_next)] = head
        spatial_next, temporal_next = spatial_next + 1 - kind, temporal_next + kind


def head_columns(ids, rank):
    return pl.ds(pl.multiple_of(ids[rank] * SIZE, SIZE), SIZE)


def pack_kernel(kinds, qkv, *refs):
    outs, temporal_out, ids = refs[:8], refs[8], refs[9]

    @pl.when(pl.program_id(0) == 0)
    def _():
        rank_heads(kinds, ids)

    y, core = lax.axis_index("y"), lax.axis_index("core")
    for part in range(2):
        for step in range(RING):
            to = lax.rem(y + step, RING) * 2 + lax.rem(core + part, 2)
            for head in range(2):
                outs[part * RING + step][0, head] = qkv[0, :, head_columns(ids, to * 2 + head)]
    for head in range(HEADS - SPATIAL):
        columns = head_columns(ids, SPATIAL + head)
        for piece in range(RING):
            rows = slice(piece * GROUP, (piece + 1) * GROUP)
            temporal_out[head * RING + piece, 0] = qkv[0, rows, columns]


def pack(kinds, qkv):
    outs = [shape(3, 2, ROWS, SIZE)] * 8 + [shape(FRAMES, 3, GROUP, SIZE)]
    return pl.pallas_call(
        pack_kernel,
        grid=(3,),
        out_shape=outs,
        in_specs=[SMEM, pl.BlockSpec((1, ROWS, D), lambda c: (c, 0, 0))],
        out_specs=[pl.BlockSpec((1, 2, ROWS, SIZE), lambda c: (c, 0, 0, 0))] * 8
        + [pl.BlockSpec((FRAMES, 1, GROUP, SIZE), lambda c: (0, c, 0, 0))],
        scratch_shapes=[pltpu.SMEM((HEADS,), jnp.int32)],
        compiler_params=params(56),
        cost_estimate=cost(0, 7_200_000),
        name="pack",
    )(kinds, qkv)


def attend(query, key, value_ones, keep=None):
    score = lax.dot_general(query, key, (((1,), (1,)), ((), ())), preferred_element_type=F32)
    if keep is not None:
        score = jnp.where(keep, score, -1e30)
    top = jnp.max(score, axis=1, keepdims=True)
    weight = jnp.exp2((score - top) * EXP_SCALE).astype(BF16)
    both = jnp.dot(weight, value_ones, preferred_element_type=F32)
    return (both[:, :SIZE] / both[:, SIZE:]).astype(BF16)


def spatial_kernel(first, chunks, out):
    y = lax.axis_index("y")
    ones = jnp.ones((8 * ROWS, SIZE), BF16)
    for head in range(2):
        key = jnp.concatenate([chunk[1, head] for chunk in chunks], axis=0)
        value = jnp.concatenate([chunk[2, head] for chunk in chunks], axis=0)
        value_ones = jnp.concatenate([value, ones], axis=1)
        for pair in range(2):
            steps = (pair * 2, pair * 2 + 1)
            query = jnp.concatenate([chunks[first + i][0, head] for i in steps], axis=0)
            result = attend(query, key, value_ones)
            for n, step in enumerate(steps):
                origin = lax.rem(y + RING - step, RING)
                out[origin, :, head * SIZE : (head + 1) * SIZE] = result[n * ROWS : (n + 1) * ROWS]


def spatial(chunks, part, *done):
    return pl.pallas_call(
        lambda *refs: spatial_kernel(part * RING, refs[:8], refs[-1]),
        out_shape=shape(RING, ROWS, 2 * SIZE),
        in_specs=[VMEM] * 8 + [ANY] * len(done),
        out_specs=VMEM,
        compiler_params=params(24),
        cost_estimate=cost(2_400_000_000, 3_000_000, 2_400_000),
        name="spatial",
    )(*chunks, *done)


def temporal_kernel(heads, *rest):
    out = rest[-1]
    span = 16
    count = FRAMES * span
    same = lax.broadcasted_iota(jnp.int32, (count, count), 0) % span == (
        lax.broadcasted_iota(jnp.int32, (count, count), 1) % span
    )
    ones = jnp.ones((count, SIZE), BF16)
    for piece in range(GROUP // span):
        rows = slice(piece * span, (piece + 1) * span)
        query, key, value = (heads[:, c, rows].reshape(count, SIZE) for c in range(3))
        result = attend(query, key, jnp.concatenate([value, ones], axis=1), same)
        out[:, rows] = result.reshape(FRAMES, span, SIZE)


def temporal(heads, *done):
    return pl.pallas_call(
        temporal_kernel,
        out_shape=shape(FRAMES, GROUP, SIZE),
        in_specs=[VMEM] + [ANY] * len(done),
        out_specs=VMEM,
        compiler_params=params(16),
        cost_estimate=cost(TEMPORAL_COST, 1_600_000, 800_000),
        name="temporal",
    )(heads, *done)


def after(array, *done):
    return pl.pallas_call(
        lambda *refs: None,
        out_shape=shape(*array.shape),
        in_specs=[ANY] * (1 + len(done)),
        out_specs=ANY,
        input_output_aliases={0: 0},
        compiler_params=params(4),
        cost_estimate=cost(0, 0),
        name="after",
    )(array, *done)


def join3_kernel(first, second, third, *rest):
    for i, ref in enumerate((first, second, third)):
        rest[-1][i] = ref[...]


def join3(slabs, *done):
    return pl.pallas_call(
        join3_kernel,
        out_shape=shape(3, *slabs[0].shape),
        in_specs=[VMEM] * 3 + [ANY] * len(done),
        out_specs=VMEM,
        compiler_params=params(4),
        cost_estimate=cost(0, 400_000),
        name="join3",
    )(*slabs, *done)


def join8_kernel(near, behind, ahead, *rest):
    out = rest[-1]
    z = lax.axis_index("z")
    for i in range(3):
        out[lax.rem(z + 7 + i, 8)] = near[i]
        out[lax.rem(z + 4 + i, 8)] = behind[i]
    for i in range(2):
        out[lax.rem(z + 2 + i, 8)] = ahead[i]


def join8(near, behind, ahead, *done):
    return pl.pallas_call(
        join8_kernel,
        out_shape=shape(8, *near.shape[1:]),
        in_specs=[VMEM] * 3 + [ANY] * len(done),
        out_specs=VMEM,
        compiler_params=params(4),
        cost_estimate=cost(0, 1_200_000),
        name="join8",
    )(near, behind, ahead, *done)


def relay_kernel(behind, ahead, *rest):
    rest[-2][...] = behind[:4]
    rest[-1][...] = ahead[4:]


def relay_halves(behind, ahead, *done):
    return pl.pallas_call(
        relay_kernel,
        out_shape=[shape(4, *behind.shape[1:])] * 2,
        in_specs=[VMEM] * 2 + [ANY] * len(done),
        out_specs=[VMEM] * 2,
        compiler_params=params(4),
        cost_estimate=cost(0, 1_200_000),
        name="relay_halves",
    )(behind, ahead, *done)


def arrange_kernel(own, behind, far_low, far_high, ahead, *rest):
    x = lax.axis_index("x")
    for step, block in enumerate((own, behind, None, ahead)):
        x_from = lax.rem(x + RING - step, RING)
        for z in range(8):
            rest[-1][z * RING + x_from] = (
                (far_low, far_high)[z // 4][z % 4] if step == 2 else block[z]
            )


def arrange(blocks, *done):
    return pl.pallas_call(
        arrange_kernel,
        out_shape=shape(FRAMES, 96, SHARE // 2),
        in_specs=[VMEM] * 5 + [ANY] * len(done),
        out_specs=VMEM,
        compiler_params=params(12),
        cost_estimate=cost(0, 4_800_000),
        name="arrange",
    )(*blocks, *done)


def halve_kernel(whole, low, high):
    low[...] = whole[:16]
    high[...] = whole[16:]


def halve(whole):
    return pl.pallas_call(
        halve_kernel,
        out_shape=[shape(16, GROUP, SIZE)] * 2,
        in_specs=[VMEM],
        out_specs=[VMEM] * 2,
        compiler_params=params(4),
        cost_estimate=cost(HALVE_COST, 800_000),
        name="halve",
    )(whole)


def collect_kernel(*refs):
    for slot in range(8):
        refs[9][:, :, slot * 256 : (slot + 1) * 256] = refs[slot][...]


def collect(blocks, done):
    return pl.pallas_call(
        collect_kernel,
        out_shape=shape(RING, ROWS, SPATIAL * SIZE),
        in_specs=[VMEM] * 8 + [ANY],
        out_specs=VMEM,
        compiler_params=params(12),
        cost_estimate=cost(COLLECT_COST, 6_400_000),
        name="collect",
    )(*blocks, done)


def project_spatial_kernel(kinds, weight, tokens, total, weight_temporal, ids, held):
    y, core = lax.axis_index("y"), lax.axis_index("core")
    rank_heads(kinds, ids)
    slot = 0
    for step in range(RING):
        origin = lax.rem(y + RING - step, RING)
        for part in range(2):
            first = origin * 4 + lax.rem(core + part, 2) * 2
            for rank in (first, first + 1):
                held[slot * SIZE : (slot + 1) * SIZE] = weight[head_columns(ids, rank)]
                slot += 1
    for head in range(HEADS - SPATIAL):
        rows = slice(head * SIZE, (head + 1) * SIZE)
        weight_temporal[rows] = weight[head_columns(ids, SPATIAL + head)]
    left = tokens[...].reshape(RING * ROWS, SPATIAL * SIZE)
    product = jnp.dot(left, held[...], preferred_element_type=F32)
    total[...] = product.reshape(RING, ROWS, SHARE // 2)


def project_spatial(kinds, weight, tokens):
    half = SHARE // 2
    return pl.pallas_call(
        project_spatial_kernel,
        out_shape=[shape(RING, ROWS, half, dtype=F32), shape(D - SPATIAL * SIZE, half)],
        in_specs=[SMEM] + [VMEM] * 2,
        out_specs=[VMEM, VMEM],
        scratch_shapes=[
            pltpu.SMEM((HEADS,), jnp.int32),
            pltpu.VMEM((SPATIAL * SIZE, half), BF16),
        ],
        compiler_params=params(20),
        cost_estimate=cost(1_200_000_000, 6_000_000),
        name="project_spatial",
    )(kinds, weight, tokens)


def project_temporal_kernel(total_own, total_other, weight_own, weight_other, *refs):
    ins, outs = refs[:8], refs[8:]
    y, core = lax.axis_index("y"), lax.axis_index("core")
    for step in (2, 1, 3, 0):
        origin = lax.rem(y + RING - step, RING)
        heads = []
        for half in ins[2 * step : 2 * step + 2]:
            heads += [half[h * 4 : h * 4 + 4].reshape(ROWS, SIZE) for h in range(4)]
        left = jnp.concatenate(heads, axis=1)
        for part, (total, weight) in enumerate(
            ((total_own, weight_own), (total_other, weight_other))
        ):
            start = pl.multiple_of(lax.rem(core + part, 2) * (SHARE // 2), SIZE)
            columns = pl.ds(start, SHARE // 2)
            product = jnp.dot(left, weight[...], preferred_element_type=F32)
            result = (total[origin] + product).astype(BF16)
            if step == 2:
                outs[3][:, columns] = result[: ROWS // 2]
                outs[4][:, columns] = result[ROWS // 2 :]
            else:
                outs[(0, 1, None, 2)[step]][:, columns] = result


def project_temporal(own, other, halves):
    whole, half = shape(ROWS, SHARE), shape(ROWS // 2, SHARE)
    return pl.pallas_call(
        project_temporal_kernel,
        out_shape=[whole, whole, whole, half, half],
        in_specs=[VMEM] * 12,
        out_specs=[VMEM] * 5,
        compiler_params=params(24),
        cost_estimate=cost(1_200_000_000, 7_000_000),
        name="project_temporal",
    )(own[0], other[0], own[1], other[1], *halves)


def finish_kernel(own, behind, ahead, far_low, far_high, out):
    y = lax.axis_index("y")
    half = ROWS // 2

    def columns(step):
        return pl.ds(pl.multiple_of(lax.rem(y + RING - step, RING) * SHARE, SIZE), SHARE)

    out[:, columns(0)] = own[...]
    out[:, columns(1)] = behind[...]
    out[:, columns(3)] = ahead[...]
    out[:half, columns(2)] = far_low[...]
    out[half:, columns(2)] = far_high[...]


def finish(*blocks):
    return pl.pallas_call(
        finish_kernel,
        out_shape=shape(ROWS, D),
        in_specs=[VMEM] * 5,
        out_specs=VMEM,
        compiler_params=params(8),
        cost_estimate=cost(0, 2_400_000),
        name="finish",
    )(*blocks)


def hop(array, axis, steps):
    size = lax.axis_size(axis)
    return lax.ppermute(array, axis, [(i, (i + steps) % size) for i in range(size)])


def hop_over(array, steps):
    perm = [
        (y * 2 + core, ((y + steps) % RING) * 2 + 1 - core)
        for y in range(RING)
        for core in range(2)
    ]
    return lax.ppermute(array, POS, perm)


def weight_slab(out_weight):
    sent = jnp.transpose(out_weight.reshape(12, 8, SHARE // 2), (1, 0, 2))
    return lax.all_to_all(sent, POS, 0, 0, tiled=True).reshape(96, SHARE // 2)


def shards(qkv, head_kind, out_weight):
    qkv = qkv.reshape(3, ROWS, D)
    slab = weight_slab(out_weight)
    packed = pack(head_kind, qkv)
    across = lax.all_to_all(packed[8], ("z", "x"), 0, 0, tiled=True)
    far_same, far_cross = hop(packed[2], "y", 1), hop(packed[6], "y", -1)
    chunks = [
        packed[0],
        hop(packed[1], "y", 1),
        hop(far_same, "y", 1),
        hop(packed[3], "y", -1),
        hop(packed[4], "core", 1),
        hop_over(packed[5], 1),
        hop_over(far_cross, -1),
        hop_over(packed[7], -1),
    ]
    slab = after(slab, far_same, far_cross)
    near = join3([hop(slab, "z", 1), slab, hop(slab, "z", -1)], *chunks[1:])
    near_behind, near_ahead = hop(near, "z", 3), hop(near, "z", -3)

    other = spatial(chunks, 1, near)
    theirs = hop(other, "core", 1)
    mine = spatial(chunks, 0, theirs)
    mine_behind, mine_ahead = hop(mine, "y", 1), hop(mine, "y", -1)
    theirs_behind, theirs_ahead = hop(theirs, "y", 1), hop(theirs, "y", -1)
    mine_far = hop(mine_behind, "y", 1)
    theirs_far = hop(theirs_ahead, "y", -1)
    results = temporal(across, mine_behind, mine_ahead)
    back = lax.all_to_all(results, ("z", "x"), 0, 0, tiled=True)

    slabs = join8(near, near_behind, near_ahead, results)
    w_behind, w_ahead = hop(slabs, "x", 1), hop(slabs, "x", -1)
    w_low, w_high = relay_halves(w_behind, w_ahead, mine_behind, mine_ahead, theirs_behind, theirs_ahead)
    w_low, w_high = hop(w_low, "x", 1), hop(w_high, "x", -1)
    weight_own = arrange((slabs, w_behind, w_low, w_high, w_ahead), mine_far, theirs_far)
    weight_own = weight_own.reshape(D, SHARE // 2)
    weight_other = hop(weight_own, "core", 1)

    low, high = halve(back)
    low_behind, high_ahead = hop(low, "y", 1), hop(high, "y", -1)
    high_behind, low_ahead = hop(high, "y", 1), hop(low, "y", -1)
    low_far, high_far = hop(low_behind, "y", 1), hop(high_ahead, "y", -1)

    blocks = [mine, theirs, mine_behind, theirs_behind, mine_far, theirs_far, mine_ahead, theirs_ahead]
    tokens = collect(blocks, weight_own)
    own = project_spatial(head_kind, weight_own, tokens)
    over = project_spatial(head_kind, weight_other, tokens)
    halves = [low, high, low_behind, high_behind, low_far, high_far, low_ahead, high_ahead]
    out_own, out_behind, out_ahead, out_low, out_high = project_temporal(own, over, halves)
    low, high = hop(out_low, "y", 1), hop(out_high, "y", -1)
    from_ahead, from_behind = hop(out_behind, "y", -1), hop(out_ahead, "y", 1)
    low, high = hop(low, "y", 1), hop(high, "y", -1)
    return finish(out_own, from_behind, from_ahead, low, high).reshape(1, ROWS, D)


def solution(mesh):
    split = Mesh(mesh.devices.reshape(8, 4, 4, 2), ("z", "x", "y", "core"))
    placed = (P(None, ("z", "x"), POS, None), P(), P(("z", "x", "y", "core"), None))
    return jax.shard_map(
        shards, mesh=split, in_specs=placed, out_specs=P(("z", "x"), POS, None), check_vma=False
    )
```

```python
import jax
import jax.numpy as jnp
from jax import lax
from jax.experimental import pallas as pl
from jax.experimental.pallas import tpu as pltpu
from jax.sharding import Mesh, PartitionSpec as P

HEADS = 24
SIZE = 128
SPATIAL = 16
D = 3072
FRAMES = 32
ROWS = 192
RING = 4
SHARE = D // RING
GROUP = 48
EXP_SCALE = 1.4426950408889634 * SIZE ** -0.5
POS = ("y", "core")
BF16 = jnp.bfloat16
F32 = jnp.float32
TEMPORAL_COST = 600_000_000
HALVE_COST = 40_000_000_000
COLLECT_COST = 40_000_000_000
VMEM = pl.BlockSpec(memory_space=pltpu.VMEM)
SMEM = pl.BlockSpec(memory_space=pltpu.SMEM)
ANY = pl.BlockSpec(memory_space=pl.ANY)


def shape(*dims, dtype=BF16):
    return jax.ShapeDtypeStruct(dims, dtype)


def params(mebibytes):
    return pltpu.CompilerParams(vmem_limit_bytes=mebibytes * 1024 * 1024)


def cost(flops, nbytes, exps=0):
    return pl.CostEstimate(flops=flops, bytes_accessed=nbytes, transcendentals=exps)


def rank_heads(kinds, ids):
    spatial_next, temporal_next = jnp.int32(0), jnp.int32(SPATIAL)
    for head in range(HEADS):
        kind = kinds[head]
        ids[jnp.where(kind == 0, spatial_next, temporal_next)] = head
        spatial_next, temporal_next = spatial_next + 1 - kind, temporal_next + kind


def head_columns(ids, rank):
    return pl.ds(pl.multiple_of(ids[rank] * SIZE, SIZE), SIZE)


def pack_kernel(kinds, qkv, *refs):
    outs, temporal_out, ids = refs[:8], refs[8], refs[9]

    @pl.when(pl.program_id(0) == 0)
    def _():
        rank_heads(kinds, ids)

    y, core = lax.axis_index("y"), lax.axis_index("core")
    for part in range(2):
        for step in range(RING):
            to = lax.rem(y + step, RING) * 2 + lax.rem(core + part, 2)
            for head in range(2):
                outs[part * RING + step][0, head] = qkv[0, :, head_columns(ids, to * 2 + head)]
    for head in range(HEADS - SPATIAL):
        columns = head_columns(ids, SPATIAL + head)
        for piece in range(RING):
            rows = slice(piece * GROUP, (piece + 1) * GROUP)
            temporal_out[head * RING + piece, 0] = qkv[0, rows, columns]


def pack(kinds, qkv):
    outs = [shape(3, 2, ROWS, SIZE)] * 8 + [shape(FRAMES, 3, GROUP, SIZE)]
    return pl.pallas_call(
        pack_kernel,
        grid=(3,),
        out_shape=outs,
        in_specs=[SMEM, pl.BlockSpec((1, ROWS, D), lambda c: (c, 0, 0))],
        out_specs=[pl.BlockSpec((1, 2, ROWS, SIZE), lambda c: (c, 0, 0, 0))] * 8
        + [pl.BlockSpec((FRAMES, 1, GROUP, SIZE), lambda c: (0, c, 0, 0))],
        scratch_shapes=[pltpu.SMEM((HEADS,), jnp.int32)],
        compiler_params=params(56),
        cost_estimate=cost(0, 7_200_000),
        name="pack",
    )(kinds, qkv)


def attend(query, key, value_ones, keep=None):
    score = lax.dot_general(query, key, (((1,), (1,)), ((), ())), preferred_element_type=F32)
    if keep is not None:
        score = jnp.where(keep, score, -1e30)
    top = jnp.max(score, axis=1, keepdims=True)
    weight = jnp.exp2((score - top) * EXP_SCALE).astype(BF16)
    both = jnp.dot(weight, value_ones, preferred_element_type=F32)
    return (both[:, :SIZE] / both[:, SIZE:]).astype(BF16)


def spatial_kernel(first, chunks, out):
    y = lax.axis_index("y")
    ones = jnp.ones((8 * ROWS, SIZE), BF16)
    for head in range(2):
        key = jnp.concatenate([chunk[1, head] for chunk in chunks], axis=0)
        value = jnp.concatenate([chunk[2, head] for chunk in chunks], axis=0)
        value_ones = jnp.concatenate([value, ones], axis=1)
        for pair in range(2):
            steps = (pair * 2, pair * 2 + 1)
            query = jnp.concatenate([chunks[first + i][0, head] for i in steps], axis=0)
            result = attend(query, key, value_ones)
            for n, step in enumerate(steps):
                origin = lax.rem(y + RING - step, RING)
                out[origin, :, head * SIZE : (head + 1) * SIZE] = result[n * ROWS : (n + 1) * ROWS]


def spatial(chunks, part, *done):
    return pl.pallas_call(
        lambda *refs: spatial_kernel(part * RING, refs[:8], refs[-1]),
        out_shape=shape(RING, ROWS, 2 * SIZE),
        in_specs=[VMEM] * 8 + [ANY] * len(done),
        out_specs=VMEM,
        compiler_params=params(24),
        cost_estimate=cost(2_400_000_000, 3_000_000, 2_400_000),
        name="spatial",
    )(*chunks, *done)


def temporal_kernel(heads, *rest):
    out = rest[-1]
    span = 16
    count = FRAMES * span
    same = lax.broadcasted_iota(jnp.int32, (count, count), 0) % span == (
        lax.broadcasted_iota(jnp.int32, (count, count), 1) % span
    )
    ones = jnp.ones((count, SIZE), BF16)
    for piece in range(GROUP // span):
        rows = slice(piece * span, (piece + 1) * span)
        query, key, value = (heads[:, c, rows].reshape(count, SIZE) for c in range(3))
        result = attend(query, key, jnp.concatenate([value, ones], axis=1), same)
        out[:, rows] = result.reshape(FRAMES, span, SIZE)


def temporal(heads, *done):
    return pl.pallas_call(
        temporal_kernel,
        out_shape=shape(FRAMES, GROUP, SIZE),
        in_specs=[VMEM] + [ANY] * len(done),
        out_specs=VMEM,
        compiler_params=params(16),
        cost_estimate=cost(TEMPORAL_COST, 1_600_000, 800_000),
        name="temporal",
    )(heads, *done)


def after(array, *done):
    return pl.pallas_call(
        lambda *refs: None,
        out_shape=shape(*array.shape),
        in_specs=[ANY] * (1 + len(done)),
        out_specs=ANY,
        input_output_aliases={0: 0},
        compiler_params=params(4),
        cost_estimate=cost(0, 0),
        name="after",
    )(array, *done)


def join3_kernel(first, second, third, *rest):
    for i, ref in enumerate((first, second, third)):
        rest[-1][i] = ref[...]


def join3(slabs, *done):
    return pl.pallas_call(
        join3_kernel,
        out_shape=shape(3, *slabs[0].shape),
        in_specs=[VMEM] * 3 + [ANY] * len(done),
        out_specs=VMEM,
        compiler_params=params(4),
        cost_estimate=cost(0, 400_000),
        name="join3",
    )(*slabs, *done)


def join8_kernel(near, behind, ahead, *rest):
    out = rest[-1]
    z = lax.axis_index("z")
    for i in range(3):
        out[lax.rem(z + 7 + i, 8)] = near[i]
        out[lax.rem(z + 4 + i, 8)] = behind[i]
    for i in range(2):
        out[lax.rem(z + 2 + i, 8)] = ahead[i]


def join8(near, behind, ahead, *done):
    return pl.pallas_call(
        join8_kernel,
        out_shape=shape(8, *near.shape[1:]),
        in_specs=[VMEM] * 3 + [ANY] * len(done),
        out_specs=VMEM,
        compiler_params=params(4),
        cost_estimate=cost(0, 1_200_000),
        name="join8",
    )(near, behind, ahead, *done)


def relay_kernel(behind, ahead, *rest):
    rest[-2][...] = behind[:4]
    rest[-1][...] = ahead[4:]


def relay_halves(behind, ahead, *done):
    return pl.pallas_call(
        relay_kernel,
        out_shape=[shape(4, *behind.shape[1:])] * 2,
        in_specs=[VMEM] * 2 + [ANY] * len(done),
        out_specs=[VMEM] * 2,
        compiler_params=params(4),
        cost_estimate=cost(0, 1_200_000),
        name="relay_halves",
    )(behind, ahead, *done)


def arrange_kernel(own, behind, far_low, far_high, ahead, *rest):
    x = lax.axis_index("x")
    for step, block in enumerate((own, behind, None, ahead)):
        x_from = lax.rem(x + RING - step, RING)
        for z in range(8):
            rest[-1][z * RING + x_from] = (
                (far_low, far_high)[z // 4][z % 4] if step == 2 else block[z]
            )


def arrange(blocks, *done):
    return pl.pallas_call(
        arrange_kernel,
        out_shape=shape(FRAMES, 96, SHARE // 2),
        in_specs=[VMEM] * 5 + [ANY] * len(done),
        out_specs=VMEM,
        compiler_params=params(12),
        cost_estimate=cost(0, 4_800_000),
        name="arrange",
    )(*blocks, *done)


def halve_kernel(whole, low, high):
    low[...] = whole[:16]
    high[...] = whole[16:]


def halve(whole):
    return pl.pallas_call(
        halve_kernel,
        out_shape=[shape(16, GROUP, SIZE)] * 2,
        in_specs=[VMEM],
        out_specs=[VMEM] * 2,
        compiler_params=params(4),
        cost_estimate=cost(HALVE_COST, 800_000),
        name="halve",
    )(whole)


def collect_kernel(*refs):
    for slot in range(8):
        refs[9][:, :, slot * 256 : (slot + 1) * 256] = refs[slot][...]


def collect(blocks, done):
    return pl.pallas_call(
        collect_kernel,
        out_shape=shape(RING, ROWS, SPATIAL * SIZE),
        in_specs=[VMEM] * 8 + [ANY],
        out_specs=VMEM,
        compiler_params=params(12),
        cost_estimate=cost(COLLECT_COST, 6_400_000),
        name="collect",
    )(*blocks, done)


def project_spatial_kernel(kinds, weight, tokens, total, weight_temporal, ids, held):
    y, core = lax.axis_index("y"), lax.axis_index("core")
    rank_heads(kinds, ids)
    slot = 0
    for step in range(RING):
        origin = lax.rem(y + RING - step, RING)
        for part in range(2):
            first = origin * 4 + lax.rem(core + part, 2) * 2
            for rank in (first, first + 1):
                held[slot * SIZE : (slot + 1) * SIZE] = weight[head_columns(ids, rank)]
                slot += 1
    for head in range(HEADS - SPATIAL):
        rows = slice(head * SIZE, (head + 1) * SIZE)
        weight_temporal[rows] = weight[head_columns(ids, SPATIAL + head)]
    left = tokens[...].reshape(RING * ROWS, SPATIAL * SIZE)
    product = jnp.dot(left, held[...], preferred_element_type=F32)
    total[...] = product.reshape(RING, ROWS, SHARE // 2)


def project_spatial(kinds, weight, tokens):
    half = SHARE // 2
    return pl.pallas_call(
        project_spatial_kernel,
        out_shape=[shape(RING, ROWS, half, dtype=F32), shape(D - SPATIAL * SIZE, half)],
        in_specs=[SMEM] + [VMEM] * 2,
        out_specs=[VMEM, VMEM],
        scratch_shapes=[
            pltpu.SMEM((HEADS,), jnp.int32),
            pltpu.VMEM((SPATIAL * SIZE, half), BF16),
        ],
        compiler_params=params(20),
        cost_estimate=cost(1_200_000_000, 6_000_000),
        name="project_spatial",
    )(kinds, weight, tokens)


def project_temporal_kernel(total_own, total_other, weight_own, weight_other, *refs):
    ins, out = refs[:8], refs[8]
    y, core = lax.axis_index("y"), lax.axis_index("core")
    for step in range(RING):
        origin = lax.rem(y + RING - step, RING)
        heads = []
        for half in ins[2 * step : 2 * step + 2]:
            heads += [half[h * 4 : h * 4 + 4].reshape(ROWS, SIZE) for h in range(4)]
        left = jnp.concatenate(heads, axis=1)
        for part, (total, weight) in enumerate(
            ((total_own, weight_own), (total_other, weight_other))
        ):
            start = pl.multiple_of(lax.rem(core + part, 2) * (SHARE // 2), SIZE)
            product = jnp.dot(left, weight[...], preferred_element_type=F32)
            out[origin, :, pl.ds(start, SHARE // 2)] = (total[origin] + product).astype(BF16)


def project_temporal(own, other, halves):
    return pl.pallas_call(
        project_temporal_kernel,
        out_shape=shape(RING, ROWS, SHARE),
        in_specs=[VMEM] * 12,
        out_specs=VMEM,
        compiler_params=params(24),
        cost_estimate=cost(1_200_000_000, 7_000_000),
        name="project_temporal",
    )(own[0], other[0], own[1], other[1], *halves)


def finish_kernel(blocks, out):
    for y in range(RING):
        out[:, y * SHARE : (y + 1) * SHARE] = blocks[y]


def finish(blocks):
    return pl.pallas_call(
        finish_kernel,
        out_shape=shape(ROWS, D),
        in_specs=[VMEM],
        out_specs=VMEM,
        compiler_params=params(8),
        cost_estimate=cost(0, 2_400_000),
        name="finish",
    )(blocks)


def hop(array, axis, steps):
    size = lax.axis_size(axis)
    return lax.ppermute(array, axis, [(i, (i + steps) % size) for i in range(size)])


def hop_over(array, steps):
    perm = [
        (y * 2 + core, ((y + steps) % RING) * 2 + 1 - core)
        for y in range(RING)
        for core in range(2)
    ]
    return lax.ppermute(array, POS, perm)


def weight_slab(out_weight):
    sent = jnp.transpose(out_weight.reshape(12, 8, SHARE // 2), (1, 0, 2))
    return lax.all_to_all(sent, POS, 0, 0, tiled=True).reshape(96, SHARE // 2)


def shards(qkv, head_kind, out_weight):
    qkv = qkv.reshape(3, ROWS, D)
    slab = weight_slab(out_weight)
    packed = pack(head_kind, qkv)
    across = lax.all_to_all(packed[8], ("z", "x"), 0, 0, tiled=True)
    far_same, far_cross = hop(packed[2], "y", 1), hop(packed[6], "y", -1)
    chunks = [
        packed[0],
        hop(packed[1], "y", 1),
        hop(far_same, "y", 1),
        hop(packed[3], "y", -1),
        hop(packed[4], "core", 1),
        hop_over(packed[5], 1),
        hop_over(far_cross, -1),
        hop_over(packed[7], -1),
    ]
    slab = after(slab, far_same, far_cross)
    near = join3([hop(slab, "z", 1), slab, hop(slab, "z", -1)], *chunks[1:])
    near_behind, near_ahead = hop(near, "z", 3), hop(near, "z", -3)

    other = spatial(chunks, 1, near)
    theirs = hop(other, "core", 1)
    mine = spatial(chunks, 0, theirs)
    mine_behind, mine_ahead = hop(mine, "y", 1), hop(mine, "y", -1)
    theirs_behind, theirs_ahead = hop(theirs, "y", 1), hop(theirs, "y", -1)
    mine_far = hop(mine_behind, "y", 1)
    theirs_far = hop(theirs_ahead, "y", -1)
    results = temporal(across, mine_behind, mine_ahead)
    back = lax.all_to_all(results, ("z", "x"), 0, 0, tiled=True)

    slabs = join8(near, near_behind, near_ahead, results)
    w_behind, w_ahead = hop(slabs, "x", 1), hop(slabs, "x", -1)
    w_low, w_high = relay_halves(w_behind, w_ahead, mine_behind, mine_ahead, theirs_behind, theirs_ahead)
    w_low, w_high = hop(w_low, "x", 1), hop(w_high, "x", -1)
    weight_own = arrange((slabs, w_behind, w_low, w_high, w_ahead), mine_far, theirs_far)
    weight_own = weight_own.reshape(D, SHARE // 2)
    weight_other = hop(weight_own, "core", 1)

    low, high = halve(back)
    low_behind, high_ahead = hop(low, "y", 1), hop(high, "y", -1)
    high_behind, low_ahead = hop(high, "y", 1), hop(low, "y", -1)
    low_far, high_far = hop(low_behind, "y", 1), hop(high_ahead, "y", -1)

    blocks = [mine, theirs, mine_behind, theirs_behind, mine_far, theirs_far, mine_ahead, theirs_ahead]
    tokens = collect(blocks, weight_own)
    own = project_spatial(head_kind, weight_own, tokens)
    over = project_spatial(head_kind, weight_other, tokens)
    halves = [low, high, low_behind, high_behind, low_far, high_far, low_ahead, high_ahead]
    out = project_temporal(own, over, halves)
    return finish(lax.all_to_all(out, "y", 0, 0, tiled=True)).reshape(1, ROWS, D)


def solution(mesh):
    split = Mesh(mesh.devices.reshape(8, 4, 4, 2), ("z", "x", "y", "core"))
    placed = (P(None, ("z", "x"), POS, None), P(), P(("z", "x", "y", "core"), None))
    return jax.shard_map(
        shards, mesh=split, in_specs=placed, out_specs=P(("z", "x"), POS, None), check_vma=False
    )
```
